32 devices in a mesh: row: 8 (over z, x), col: 4 (over y, core).
Axes of the slice: x: 2, y: 2, z: 4, core: 2. Of those that a mesh axis runs over, the one named last changes fastest.
Arguments:
- sp2_branch: int32 [3], replicated, may hold values from 0 to 1, as said below
- p0_occupancy: int32 [8, 8], replicated, may hold values from 0 to 1, as said below
- p1_occupancy: int32 [8, 8], replicated, may hold values from 0 to 1, as said below
- p0_columns: bfloat16 [6144, 512], P('col'), as said below
- p1_tiles: bfloat16 [3, 2048, 2048], P(None, 'row', 'col'), may hold values from -6 to 6, as said below
Outputs:
- p1_next: bfloat16 [3, 2048, 2048], P(None, 'row', 'col')
The draws below stay inside these ranges and needn't reach their ends.
Inputs may be any that keep to these rules, and one draw needn't show every extreme that they name: `sp2_branch`: both values occur among the displacements. `p0_occupancy`: symmetric; every diagonal block is 1; blocks more than 2 apart around the circle of 8 blocks are 0. `p1_occupancy`: symmetric. `p0_columns`: the strips describe one symmetric matrix: a stored entry at row u and column v equals the stored entry at row v and column u; blocks more than 2 apart around the circle are zero. `p1_tiles`: each displacement's matrix is symmetric.
All inputs are finite; a program needn't handle non-finite values.
Results may differ from the reference program's by a relative error of at most 0.001.
Values may be sent and summed in bfloat16 or wider, within the bound.
A program may use at most 192 MiB of HBM per device.

```python
import jax
import jax.numpy as jnp
import numpy as np
from jax import lax

DISP = 3
BLK = 256
COLB = 2
BLOCKS = 8
ROWB = 1
HALF = 2
CW = 512
RH = 256
ORDER = 2048
STRIP = 1536
RSTRIP = 1280
N_ROW = 8
N_COL = 4


def draw_sp2_branch(key, part):
    key_first, key_rest, key_order = jax.random.split(jax.random.fold_in(key, 37), 3)
    first = jax.random.randint(key_first, (1,), 0, 2).astype(jnp.int32)
    rest = jax.random.randint(key_rest, (DISP - 2,), 0, 2).astype(jnp.int32)
    values = jnp.concatenate([first, 1 - first, rest]).astype(jnp.int32)
    order = jax.random.permutation(key_order, DISP)
    return values[order].astype(jnp.int32)


def draw_p0_columns(key, part):
    key_upper, key_diag = jax.random.split(jax.random.fold_in(key, 17))
    groups = BLOCKS // COLB
    span_rows = COLB + 2 * HALF
    upper = jax.random.normal(key_upper, (BLOCKS, HALF + 1, BLK, BLK), jnp.float32) * 0.02
    diag_vals = jax.random.uniform(key_diag, (BLOCKS, BLK), jnp.float32, 0.2, 0.8)
    group_ids = np.arange(groups)[:, None, None]
    row_ids = np.arange(span_rows)[None, :, None]
    col_ids = np.arange(COLB)[None, None, :]
    shape = (groups, span_rows, COLB)
    col_block = np.broadcast_to(group_ids * COLB + col_ids, shape)
    row_block = np.broadcast_to((group_ids * COLB - HALF + row_ids) % BLOCKS, shape)
    offset = np.broadcast_to(row_ids - HALF - col_ids, shape)
    below = upper[col_block, np.clip(offset, 0, HALF)]
    above = jnp.swapaxes(upper[row_block, np.clip(-offset, 0, HALF)], -1, -2)
    eye_table = np.eye(BLK, dtype=np.float32)
    centre = 0.5 * (below + jnp.swapaxes(below, -1, -2)) + eye_table[None, None, None] * diag_vals[col_block][:, :, :, None, :]
    off_pos = jnp.asarray(offset > 0)[:, :, :, None, None]
    off_neg = jnp.asarray(offset < 0)[:, :, :, None, None]
    inside = jnp.asarray(np.abs(offset) <= HALF)[:, :, :, None, None]
    tiles = jnp.where(off_pos, below, jnp.where(off_neg, above, centre))
    tiles = jnp.where(inside, tiles, 0.0)
    strip = tiles.transpose(0, 1, 3, 2, 4).reshape(groups * span_rows * BLK, COLB * BLK)
    return strip.astype(jnp.bfloat16)


def draw_p0_occupancy(key, part):
    bits = jax.random.randint(jax.random.fold_in(key, 23), (BLOCKS, BLOCKS), 0, 4)
    rows = jnp.arange(BLOCKS, dtype=jnp.int32)[:, None]
    cols = jnp.arange(BLOCKS, dtype=jnp.int32)[None, :]
    sym = jnp.where(rows <= cols, bits, bits.T)
    dist = jnp.minimum((rows - cols) % BLOCKS, (cols - rows) % BLOCKS)
    occupied = (sym > 0).astype(jnp.int32)
    return jnp.where(dist == 0, 1, jnp.where(dist <= HALF, occupied, 0)).astype(jnp.int32)


def draw_p1_occupancy(key, part):
    key_atom, key_bits = jax.random.split(jax.random.fold_in(key, 29))
    atom = jax.random.randint(key_atom, (), 0, BLOCKS)
    bits = jax.random.randint(key_bits, (BLOCKS, BLOCKS), 0, 2)
    rows = jnp.arange(BLOCKS, dtype=jnp.int32)[:, None]
    cols = jnp.arange(BLOCKS, dtype=jnp.int32)[None, :]
    sym = jnp.where(rows <= cols, bits, bits.T)
    ids = jnp.arange(BLOCKS, dtype=jnp.int32)
    dist = jnp.minimum((ids - atom) % BLOCKS, (atom - ids) % BLOCKS)
    near_row = (dist <= BLOCKS // 8)[:, None]
    near_col = (dist <= BLOCKS // 8)[None, :]
    return jnp.where(near_row | near_col, 1, sym).astype(jnp.int32)


def draw_p1_tiles(key, part):
    base_key = jax.random.fold_in(key, 31)
    base = jax.random.normal(base_key, (DISP, ORDER, ORDER), jnp.float32)
    sym = (base + jnp.swapaxes(base, -1, -2)) * 0.7071
    return jnp.clip(sym, -6.0, 6.0).astype(jnp.bfloat16)


def setup_inputs(seed: int = 0) -> dict:
    key_of = jax.random.split(jax.random.key(seed), 6)
    sp2_branch = draw_sp2_branch(jax.random.fold_in(key_of[5], 71), 0)
    p0_occupancy = draw_p0_occupancy(jax.random.fold_in(key_of[5], 71), 0)
    p1_occupancy = draw_p1_occupancy(jax.random.fold_in(key_of[5], 71), 0)
    p0_columns = draw_p0_columns(jax.random.fold_in(key_of[5], 71), 0)
    p1_tiles = draw_p1_tiles(jax.random.fold_in(key_of[5], 71), 0)
    return dict(sp2_branch=sp2_branch, p0_occupancy=p0_occupancy, p1_occupancy=p1_occupancy, p0_columns=p0_columns, p1_tiles=p1_tiles)


def mask_blocks(values, occupancy):
    leading = values.shape[:-2]
    row_blocks = values.shape[-2] // BLK
    col_blocks = values.shape[-1] // BLK
    shaped = values.reshape(leading + (row_blocks, BLK, col_blocks, BLK))
    weight = occupancy.astype(values.dtype)[:, None, :, None]
    return (shaped * weight).reshape(values.shape)


def reference(sp2_branch, p0_occupancy, p1_occupancy, p0_columns, p1_tiles):
    strips = p0_columns.reshape(N_COL, STRIP, CW)
    group_ids = jnp.arange(N_COL, dtype=jnp.int32)
    strip_rows = (group_ids[:, None] * COLB - HALF + jnp.arange(COLB + 2 * HALF, dtype=jnp.int32)[None, :]) % BLOCKS
    strip_cols = group_ids[:, None] * COLB + jnp.arange(COLB, dtype=jnp.int32)[None, :]
    strip_occ = p0_occupancy[strip_rows[:, :, None], strip_cols[:, None, :]]
    strips_masked = jax.vmap(mask_blocks)(strips, strip_occ)
    strips_wide = strips_masked.astype(jnp.float32)
    p1_masked = mask_blocks(p1_tiles, p1_occupancy)
    col_index = ((group_ids[:, None] * COLB - HALF) * BLK + jnp.arange(STRIP, dtype=jnp.int32)[None, :]) % ORDER

    def one_row(row_id):
        rows_now = lax.dynamic_slice_in_dim(p1_masked, (row_id * RH).astype(jnp.int32), RH, 1)
        gathered = rows_now[:, :, col_index]
        right_prod = jnp.einsum("drcs,csk->drck", gathered.astype(jnp.float32), strips_wide)
        right_prod = right_prod.reshape(DISP, RH, ORDER)
        owner_col = (row_id * ROWB) // COLB
        offset_blocks = row_id * ROWB - owner_col * COLB
        owner_strip = lax.dynamic_index_in_dim(strips_masked, owner_col.astype(jnp.int32), 0, keepdims=False)
        factor = lax.dynamic_slice(owner_strip, ((offset_blocks * BLK).astype(jnp.int32), (offset_blocks * BLK).astype(jnp.int32)), (RSTRIP, RH))
        band_rows = ((row_id * ROWB - HALF) * BLK + jnp.arange(RSTRIP, dtype=jnp.int32)) % ORDER
        picked = p1_masked[:, band_rows, :]
        left_prod = jnp.einsum("kr,dkc->drc", factor.astype(jnp.float32), picked.astype(jnp.float32))
        bracket = right_prod + left_prod
        squared = (sp2_branch == 1)[:, None, None]
        chosen = jnp.where(squared, bracket, 2.0 * rows_now.astype(jnp.float32) - bracket)
        row_occ = lax.dynamic_slice(p1_occupancy, ((row_id * ROWB).astype(jnp.int32), jnp.int32(0)), (ROWB, BLOCKS))
        return mask_blocks(chosen, row_occ).astype(jnp.bfloat16)

    stacked = lax.map(one_row, jnp.arange(N_ROW, dtype=jnp.int32))
    return stacked.transpose(1, 0, 2, 3).reshape(DISP, ORDER, ORDER)
```

```python
import functools

import jax
import jax.numpy as jnp
from jax import lax
from jax.experimental import pallas as pl
from jax.experimental.pallas import tpu as pltpu
from jax.sharding import PartitionSpec as P

BLK = 256
MESH = pl.DeviceIdType.MESH


def mask_into(dst, src, occ, row_block, col_block, total):
    rows, cols = src.shape[-2], src.shape[-1]
    for i in range(rows // BLK):
        for j in range(cols // BLK):
            weight = occ[lax.rem(row_block + i + total, total), col_block + j].astype(jnp.float32)
            at = (slice(i * BLK, (i + 1) * BLK), slice(j * BLK, (j + 1) * BLK))
            at = (slice(None),) * (len(src.shape) - 2) + at
            dst[at] = (src[at].astype(jnp.float32) * weight).astype(jnp.bfloat16)


def kernel(
    row_count, col_count, relay,
    branch, p0_occ, p1_occ, strip_in, tile_in, out,
    mine, strip, fact, acc, cols, rows,
    col_send, col_recv, row_send, row_recv, fact_send, fact_recv,
):
    disp, height, width = tile_in.shape
    row_blocks, col_blocks = height // BLK, width // BLK
    total = col_count * col_blocks
    half = (strip_in.shape[0] // BLK - col_blocks) // 2
    col_span, row_span = half // col_blocks, half // row_blocks
    r, c = lax.axis_index("row"), lax.axis_index("col")
    odd = lax.rem(r, 2)

    def row_id(distance):
        return (lax.rem(r + distance + row_count, row_count), c)

    def col_id(distance):
        return (r, lax.rem(c + distance + col_count, col_count))

    row_far = [t for t in range(-row_span, row_span + 1) if t]
    col_far = [t for t in range(-col_span, col_span + 1) if t]
    partner = row_id(1 - 2 * odd)
    greeted = [col_id(t) for t in range(1, col_count)]
    greeted += [row_id(2), row_id(-2), partner] if relay else [row_id(t) for t in row_far]
    barrier = pltpu.get_barrier_semaphore()
    for device in greeted:
        pl.semaphore_signal(barrier, inc=1, device_id=device, device_id_type=MESH)

    mask_into(mine, tile_in, p1_occ, r * row_blocks, c * col_blocks, total)
    pl.semaphore_wait(barrier, len(greeted))

    def remote(src, dst, send, recv, device):
        return pltpu.make_async_remote_copy(
            src_ref=src, dst_ref=dst, send_sem=send, recv_sem=recv,
            device_id=device, device_id_type=MESH,
        )

    def z_copy(which, d):
        return remote(mine.at[d], rows.at[3 * which, d], row_send.at[which, d],
                      row_recv.at[which, d], row_id(2 - 4 * which))

    def own_copy(d):
        return remote(mine.at[d], rows.at[1 + odd, d], row_send.at[2, d],
                      row_recv.at[2, d], partner)

    def relay_copy(d):
        return remote(rows.at[3 - 3 * odd, d], rows.at[2 - odd, d], row_send.at[3, d],
                      row_recv.at[3, d], partner)

    def row_copy(k, d):
        return remote(mine.at[d], rows.at[len(row_far) - 1 - k, d],
                      row_send.at[len(row_far) - 1 - k, d],
                      row_recv.at[len(row_far) - 1 - k, d], row_id(row_far[k]))

    def col_copy(k):
        back = len(col_far) - 1 - k
        return remote(mine, cols.at[back], col_send.at[back], col_recv.at[back],
                      col_id(col_far[k]))

    if relay:
        for d in range(disp):
            z_copy(0, d).start()
            z_copy(1, d).start()
        for d in range(disp):
            own_copy(d).start()
    else:
        for d in range(disp):
            for k in range(len(row_far)):
                row_copy(k, d).start()

    mask_into(strip, strip_in, p0_occ, c * col_blocks - half, c * col_blocks, total)
    owner = r * row_blocks // col_blocks
    offset = pl.multiple_of((r * row_blocks - owner * col_blocks) * BLK, BLK)

    def fact_copy(k):
        return remote(fact, fact, fact_send.at[k], fact_recv.at[0], col_id(k + 1))

    @pl.when(c == owner)
    def _():
        for k in range(fact.shape[1] // BLK):
            for i in range(row_blocks):
                block = strip[pl.ds(offset + k * BLK, BLK), pl.ds(offset + i * BLK, BLK)]
                fact[i * BLK:(i + 1) * BLK, k * BLK:(k + 1) * BLK] = block.T
        for k in range(col_count - 1):
            fact_copy(k).start()

    for k in range(len(col_far)):
        col_copy(k).start()

    def col_add(tile, distance, first=False):
        at = pl.ds(pl.multiple_of((distance + col_span) * width, BLK), width)

        def step(d, carry):
            term = jnp.dot(tile[d], strip[at, :], preferred_element_type=jnp.float32)
            acc[d] = term if first else acc[d] + term
            return carry

        lax.fori_loop(0, disp, step, 0)

    def row_term(tile, distance, d):
        at = pl.ds(pl.multiple_of((distance + row_span) * height, BLK), height)
        return jnp.dot(fact[:, at], tile[d], preferred_element_type=jnp.float32)

    def row_add(tile, distance):
        def step(d, carry):
            acc[d] += row_term(tile, distance, d)
            return carry

        lax.fori_loop(0, disp, step, 0)

    def finish(d):
        squared = branch[d].astype(jnp.float32)
        for i in range(row_blocks):
            for j in range(col_blocks):
                at = (d, slice(i * BLK, (i + 1) * BLK), slice(j * BLK, (j + 1) * BLK))
                weight = p1_occ[r * row_blocks + i, c * col_blocks + j].astype(jnp.float32)
                own = mine[at].astype(jnp.float32) * (2.0 - 2.0 * squared)
                value = own + acc[at] * (2.0 * squared - 1.0)
                out[at] = (value * weight).astype(jnp.bfloat16)

    def wait_fact():
        @pl.when(c != owner)
        def _():
            fact_copy(0).wait_recv()

    col_add(mine, 0, first=True)
    if relay:
        def forward(d):
            remote(mine.at[d], rows.at[0, d], row_send.at[0, d],
                   row_recv.at[1 - odd, d], partner).wait_recv()
            relay_copy(d).start()

        forward(0)
        wait_fact()
        row_add(mine, 0)
        forward(1)
        for k in range(len(col_far)):
            col_copy(len(col_far) - 1 - k).wait_recv()
            col_add(cols.at[k], col_far[k])
        for d in range(disp):
            own_copy(d).wait_recv()
        row_add(rows.at[2 - odd], 1 - 2 * odd)
        for d in range(2, disp):
            forward(d)
        row_add(rows.at[3 - 3 * odd], 2 - 4 * odd)
        for d in range(disp):
            remote(mine.at[d], rows.at[0, d], row_send.at[0, d],
                   row_recv.at[odd, d], partner).wait_recv()
        row_add(rows.at[3 * odd], 4 * odd - 2)
        for d in range(disp):
            relay_copy(d).wait_recv()
            acc[d] += row_term(rows.at[1 + odd], 2 * odd - 1, d)
            finish(d)
    else:
        wait_fact()
        row_add(mine, 0)
        for k in range(len(col_far)):
            col_copy(k).wait_recv()
            col_add(cols.at[len(col_far) - 1 - k], col_far[len(col_far) - 1 - k])
        for k in range(len(row_far)):
            for d in range(disp):
                row_copy(k, d).wait_recv()
            row_add(rows.at[len(row_far) - 1 - k], row_far[len(row_far) - 1 - k])
        for d in range(disp):
            finish(d)

    for k in range(len(col_far)):
        col_copy(k).wait_send()
    for d in range(disp):
        if relay:
            z_copy(0, d).wait_send()
            z_copy(1, d).wait_send()
            own_copy(d).wait_send()
            relay_copy(d).wait_send()
        else:
            for k in range(len(row_far)):
                row_copy(k, d).wait_send()

    @pl.when(c == owner)
    def _():
        for k in range(col_count - 1):
            fact_copy(k).wait_send()


def body(sp2_branch, p0_occupancy, p1_occupancy, p0_columns, p1_tiles):
    row_count, col_count = lax.axis_size("row"), lax.axis_size("col")
    disp, height, width = p1_tiles.shape
    strip_rows = p0_columns.shape[0]
    half = (strip_rows - width) // 2
    row_slots, col_slots = 2 * (half // height), 2 * (half // width)
    bf16 = jnp.bfloat16
    relay = row_slots == 4
    flops = 2 * disp * height * width * (strip_rows + height + 2 * half)
    return pl.pallas_call(
        functools.partial(kernel, row_count, col_count, relay),
        out_shape=jax.ShapeDtypeStruct(p1_tiles.shape, bf16),
        in_specs=[pl.BlockSpec(memory_space=pltpu.SMEM)] * 3
        + [pl.BlockSpec(memory_space=pltpu.VMEM)] * 2,
        out_specs=pl.BlockSpec(memory_space=pltpu.VMEM),
        scratch_shapes=[
            pltpu.VMEM((disp, height, width), bf16),
            pltpu.VMEM(p0_columns.shape, bf16),
            pltpu.VMEM((height, height + 2 * half), bf16),
            pltpu.VMEM((disp, height, width), jnp.float32),
            pltpu.VMEM((col_slots, disp, height, width), bf16),
            pltpu.VMEM((row_slots, disp, height, width), bf16),
            pltpu.SemaphoreType.DMA((col_slots,)),
            pltpu.SemaphoreType.DMA((col_slots,)),
            pltpu.SemaphoreType.DMA((row_slots, disp)),
            pltpu.SemaphoreType.DMA((row_slots, disp)),
            pltpu.SemaphoreType.DMA((col_count - 1,)),
            pltpu.SemaphoreType.DMA((1,)),
        ],
        compiler_params=pltpu.CompilerParams(
            collective_id=0, has_side_effects=True, vmem_limit_bytes=58 * 1024 * 1024
        ),
        cost_estimate=pl.CostEstimate(flops=flops, bytes_accessed=4 << 20, transcendentals=0),
    )(sp2_branch, p0_occupancy, p1_occupancy, p0_columns, p1_tiles)


def solution(mesh):
    in_specs = (P(), P(), P(), P("col", None), P(None, "row", "col"))
    out_specs = P(None, "row", "col")
    return jax.shard_map(body, mesh=mesh, in_specs=in_specs, out_specs=out_specs, check_vma=False)
```

```python
import functools

import jax
import jax.numpy as jnp
from jax import lax
from jax.experimental import pallas as pl
from jax.experimental.pallas import tpu as pltpu
from jax.sharding import PartitionSpec as P

BLK = 256
MESH = pl.DeviceIdType.MESH


def mask_into(dst, src, occ, row_block, col_block, total):
    rows, cols = src.shape[-2], src.shape[-1]
    for i in range(rows // BLK):
        for j in range(cols // BLK):
            weight = occ[lax.rem(row_block + i + total, total), col_block + j].astype(jnp.float32)
            at = (slice(i * BLK, (i + 1) * BLK), slice(j * BLK, (j + 1) * BLK))
            at = (slice(None),) * (len(src.shape) - 2) + at
            dst[at] = (src[at].astype(jnp.float32) * weight).astype(jnp.bfloat16)


def kernel(
    row_count, col_count, relay,
    branch, p0_occ, p1_occ, strip_in, tile_in, out,
    mine, strip, fact, acc, cols, rows,
    col_send, col_recv, row_send, row_recv, fact_send, fact_recv,
):
    disp, height, width = tile_in.shape
    row_blocks, col_blocks = height // BLK, width // BLK
    total = col_count * col_blocks
    half = (strip_in.shape[0] // BLK - col_blocks) // 2
    col_span, row_span = half // col_blocks, half // row_blocks
    r, c = lax.axis_index("row"), lax.axis_index("col")
    odd = lax.rem(r, 2)

    def row_id(distance):
        return (lax.rem(r + distance + row_count, row_count), c)

    def col_id(distance):
        return (r, lax.rem(c + distance + col_count, col_count))

    row_far = [t for t in range(-row_span, row_span + 1) if t]
    col_far = [t for t in range(-col_span, col_span + 1) if t]
    partner = row_id(1 - 2 * odd)
    greeted = [col_id(t) for t in range(1, col_count)]
    greeted += [row_id(2), row_id(-2), partner] if relay else [row_id(t) for t in row_far]
    barrier = pltpu.get_barrier_semaphore()
    for device in greeted:
        pl.semaphore_signal(barrier, inc=1, device_id=device, device_id_type=MESH)

    mask_into(mine, tile_in, p1_occ, r * row_blocks, c * col_blocks, total)
    pl.semaphore_wait(barrier, len(greeted))

    def remote(src, dst, send, recv, device):
        return pltpu.make_async_remote_copy(
            src_ref=src, dst_ref=dst, send_sem=send, recv_sem=recv,
            device_id=device, device_id_type=MESH,
        )

    def first_copy(d):
        return remote(mine.at[d], rows.at[3 - 3 * odd, d], row_send.at[0, d],
                      row_recv.at[0, d], row_id(4 * odd - 2))

    def last_copy(d):
        return remote(mine.at[d], rows.at[3 * odd, d], row_send.at[1, d],
                      row_recv.at[1, d], row_id(2 - 4 * odd))

    def own_copy(d):
        return remote(mine.at[d], rows.at[1 + odd, d], row_send.at[2, d],
                      row_recv.at[2, d], partner)

    def relay_copy(d):
        return remote(rows.at[3 - 3 * odd, d], rows.at[2 - odd, d], row_send.at[3, d],
                      row_recv.at[3, d], partner)

    def row_copy(k, d):
        return remote(mine.at[d], rows.at[len(row_far) - 1 - k, d],
                      row_send.at[len(row_far) - 1 - k, d],
                      row_recv.at[len(row_far) - 1 - k, d], row_id(row_far[k]))

    def col_copy(k):
        back = len(col_far) - 1 - k
        return remote(mine, cols.at[back], col_send.at[back], col_recv.at[back],
                      col_id(col_far[k]))

    if relay:
        for d in range(disp):
            first_copy(d).start()
            own_copy(d).start()
    else:
        for d in range(disp):
            for k in range(len(row_far)):
                row_copy(k, d).start()

    mask_into(strip, strip_in, p0_occ, c * col_blocks - half, c * col_blocks, total)
    owner = r * row_blocks // col_blocks
    offset = pl.multiple_of((r * row_blocks - owner * col_blocks) * BLK, BLK)

    def fact_copy(k):
        return remote(fact, fact, fact_send.at[k], fact_recv.at[0], col_id(k + 1))

    core_odd = lax.rem(c, 2)
    core = col_id(1 - 2 * core_odd)
    across = lax.rem(owner + 2, col_count)

    def fact_core():
        return remote(fact, fact, fact_send.at[0], fact_recv.at[0], core)

    def fact_across():
        return remote(fact, fact, fact_send.at[1], fact_recv.at[0], col_id(2))

    def col_core():
        return remote(mine, cols.at[core_odd], col_send.at[0], col_recv.at[0], core)

    def col_across():
        return remote(mine, cols.at[1 - core_odd], col_send.at[1], col_recv.at[1],
                      col_id(2 * core_odd - 1))

    @pl.when(c == owner)
    def _():
        for k in range(fact.shape[1] // BLK):
            for i in range(row_blocks):
                block = strip[pl.ds(offset + k * BLK, BLK), pl.ds(offset + i * BLK, BLK)]
                fact[i * BLK:(i + 1) * BLK, k * BLK:(k + 1) * BLK] = block.T
        if relay:
            fact_across().start()
            fact_core().start()
        else:
            for k in range(col_count - 1):
                fact_copy(k).start()

    if relay:
        col_core().start()
    else:
        for k in range(len(col_far)):
            col_copy(k).start()

    def col_add(tile, distance, first=False):
        at = pl.ds(pl.multiple_of((distance + col_span) * width, BLK), width)

        def step(d, carry):
            term = jnp.dot(tile[d], strip[at, :], preferred_element_type=jnp.float32)
            acc[d] = term if first else acc[d] + term
            return carry

        lax.fori_loop(0, disp, step, 0)

    def row_term(tile, distance, d):
        at = pl.ds(pl.multiple_of((distance + row_span) * height, BLK), height)
        return jnp.dot(fact[:, at], tile[d], preferred_element_type=jnp.float32)

    def row_add(tile, distance):
        def step(d, carry):
            acc[d] += row_term(tile, distance, d)
            return carry

        lax.fori_loop(0, disp, step, 0)

    def finish(d):
        squared = branch[d].astype(jnp.float32)
        for i in range(row_blocks):
            for j in range(col_blocks):
                at = (d, slice(i * BLK, (i + 1) * BLK), slice(j * BLK, (j + 1) * BLK))
                weight = p1_occ[r * row_blocks + i, c * col_blocks + j].astype(jnp.float32)
                own = mine[at].astype(jnp.float32) * (2.0 - 2.0 * squared)
                value = own + acc[at] * (2.0 * squared - 1.0)
                out[at] = (value * weight).astype(jnp.bfloat16)

    def wait_fact():
        @pl.when(c != owner)
        def _():
            fact_copy(0).wait_recv()

        if relay:
            @pl.when(c == across)
            def _():
                fact_core().start()

    col_add(mine, 0, first=True)
    if relay:
        def forward(d):
            first_copy(d).wait_recv()
            relay_copy(d).start()

        col_core().wait_recv()
        col_add(cols.at[1 - core_odd], 1 - 2 * core_odd)
        forward(0)
        col_across().start()
        wait_fact()
        row_add(mine, 0)
        forward(1)
        first_copy(1).wait_send()
        last_copy(0).start()
        forward(2)
        first_copy(2).wait_send()
        for d in range(1, disp):
            last_copy(d).start()
        for d in range(disp):
            own_copy(d).wait_recv()
        row_add(rows.at[2 - odd], 1 - 2 * odd)
        row_add(rows.at[3 - 3 * odd], 2 - 4 * odd)
        col_across().wait_recv()
        col_add(cols.at[core_odd], 2 * core_odd - 1)
        for d in range(disp):
            last_copy(d).wait_recv()
            acc[d] += row_term(rows.at[3 * odd], 4 * odd - 2, d)
            relay_copy(d).wait_recv()
            acc[d] += row_term(rows.at[1 + odd], 2 * odd - 1, d)
            finish(d)
    else:
        wait_fact()
        row_add(mine, 0)
        for k in range(len(col_far)):
            col_copy(k).wait_recv()
            col_add(cols.at[len(col_far) - 1 - k], col_far[len(col_far) - 1 - k])
        for k in range(len(row_far)):
            for d in range(disp):
                row_copy(k, d).wait_recv()
            row_add(rows.at[len(row_far) - 1 - k], row_far[len(row_far) - 1 - k])
        for d in range(disp):
            finish(d)

    if relay:
        col_core().wait_send()
        col_across().wait_send()
        first_copy(0).wait_send()
        for d in range(disp):
            last_copy(d).wait_send()
            own_copy(d).wait_send()
            relay_copy(d).wait_send()

        @pl.when(c == owner)
        def _():
            fact_across().wait_send()

        @pl.when(jnp.logical_or(c == owner, c == across))
        def _():
            fact_core().wait_send()
    else:
        for k in range(len(col_far)):
            col_copy(k).wait_send()
        for d in range(disp):
            for k in range(len(row_far)):
                row_copy(k, d).wait_send()

        @pl.when(c == owner)
        def _():
            for k in range(col_count - 1):
                fact_copy(k).wait_send()


def body(sp2_branch, p0_occupancy, p1_occupancy, p0_columns, p1_tiles):
    row_count, col_count = lax.axis_size("row"), lax.axis_size("col")
    disp, height, width = p1_tiles.shape
    strip_rows = p0_columns.shape[0]
    half = (strip_rows - width) // 2
    row_slots, col_slots = 2 * (half // height), 2 * (half // width)
    bf16 = jnp.bfloat16
    relay = row_slots == 4 and col_slots == 2 and col_count == 4 and disp == 3
    flops = 2 * disp * height * width * (strip_rows + height + 2 * half)
    return pl.pallas_call(
        functools.partial(kernel, row_count, col_count, relay),
        out_shape=jax.ShapeDtypeStruct(p1_tiles.shape, bf16),
        in_specs=[pl.BlockSpec(memory_space=pltpu.SMEM)] * 3
        + [pl.BlockSpec(memory_space=pltpu.VMEM)] * 2,
        out_specs=pl.BlockSpec(memory_space=pltpu.VMEM),
        scratch_shapes=[
            pltpu.VMEM((disp, height, width), bf16),
            pltpu.VMEM(p0_columns.shape, bf16),
            pltpu.VMEM((height, height + 2 * half), bf16),
            pltpu.VMEM((disp, height, width), jnp.float32),
            pltpu.VMEM((col_slots, disp, height, width), bf16),
            pltpu.VMEM((row_slots, disp, height, width), bf16),
            pltpu.SemaphoreType.DMA((col_slots,)),
            pltpu.SemaphoreType.DMA((col_slots,)),
            pltpu.SemaphoreType.DMA((row_slots, disp)),
            pltpu.SemaphoreType.DMA((row_slots, disp)),
            pltpu.SemaphoreType.DMA((col_count - 1,)),
            pltpu.SemaphoreType.DMA((1,)),
        ],
        compiler_params=pltpu.CompilerParams(
            collective_id=0, has_side_effects=True, vmem_limit_bytes=58 * 1024 * 1024
        ),
        cost_estimate=pl.CostEstimate(flops=flops, bytes_accessed=4 << 20, transcendentals=0),
    )(sp2_branch, p0_occupancy, p1_occupancy, p0_columns, p1_tiles)


def solution(mesh):
    in_specs = (P(), P(), P(), P("col", None), P(None, "row", "col"))
    out_specs = P(None, "row", "col")
    return jax.shard_map(body, mesh=mesh, in_specs=in_specs, out_specs=out_specs, check_vma=False)
```

```python
import functools

import jax
import jax.numpy as jnp
from jax import lax
from jax.experimental import pallas as pl
from jax.experimental.pallas import tpu as pltpu
from jax.sharding import PartitionSpec as P

BLK = 256
MESH = pl.DeviceIdType.MESH


def mask_blocks(values, occ, row_block, col_block, total):
    rows, cols = values.shape
    for i in range(rows // BLK):
        for j in range(cols // BLK):
            weight = occ[lax.rem(row_block + i + total, total), col_block + j].astype(jnp.float32)
            at = (slice(i * BLK, (i + 1) * BLK), slice(j * BLK, (j + 1) * BLK))
            values[at] = (values[at].astype(jnp.float32) * weight).astype(jnp.bfloat16)


def kernel(
    row_count, col_count, relay,
    branch, p0_occ, p1_occ, strip_in, tile_in, out,
    load_sem, mine, strip, fact, acc, cols, rows,
    col_send, col_recv, row_send, row_recv, fact_send, fact_recv,
):
    disp, height, width = tile_in.shape
    row_blocks, col_blocks = height // BLK, width // BLK
    total = col_count * col_blocks
    half = (strip_in.shape[0] // BLK - col_blocks) // 2
    col_span, row_span = half // col_blocks, half // row_blocks
    r, c = lax.axis_index("row"), lax.axis_index("col")
    odd = lax.rem(r, 2)

    def row_id(distance):
        return (lax.rem(r + distance + row_count, row_count), c)

    def col_id(distance):
        return (r, lax.rem(c + distance + col_count, col_count))

    row_far = [t for t in range(-row_span, row_span + 1) if t]
    col_far = [t for t in range(-col_span, col_span + 1) if t]
    partner = row_id(1 - 2 * odd)
    greeted = [col_id(t) for t in range(1, col_count)]
    greeted += [row_id(2), row_id(-2), partner] if relay else [row_id(t) for t in row_far]
    barrier = pltpu.get_barrier_semaphore()
    for device in greeted:
        pl.semaphore_signal(barrier, inc=1, device_id=device, device_id_type=MESH)

    loads = [pltpu.make_async_copy(tile_in.at[d], mine.at[d], load_sem.at[d]) for d in range(disp)]
    loads.append(pltpu.make_async_copy(strip_in, strip, load_sem.at[disp]))
    for load in loads:
        load.start()

    def load_tile(d):
        loads[d].wait()
        mask_blocks(mine.at[d], p1_occ, r * row_blocks, c * col_blocks, total)

    def remote(src, dst, send, recv, device):
        return pltpu.make_async_remote_copy(
            src_ref=src, dst_ref=dst, send_sem=send, recv_sem=recv,
            device_id=device, device_id_type=MESH,
        )

    def first_copy(d):
        return remote(mine.at[d], rows.at[3 - 3 * odd, d], row_send.at[0, d],
                      row_recv.at[0, d], row_id(4 * odd - 2))

    def last_copy(d):
        return remote(mine.at[d], rows.at[3 * odd, d], row_send.at[1, d],
                      row_recv.at[1, d], row_id(2 - 4 * odd))

    def own_copy(d):
        return remote(mine.at[d], rows.at[1 + odd, d], row_send.at[2, d],
                      row_recv.at[2, d], partner)

    def relay_copy(d):
        return remote(rows.at[3 - 3 * odd, d], rows.at[2 - odd, d], row_send.at[3, d],
                      row_recv.at[3, d], partner)

    def row_copy(k, d):
        return remote(mine.at[d], rows.at[len(row_far) - 1 - k, d],
                      row_send.at[len(row_far) - 1 - k, d],
                      row_recv.at[len(row_far) - 1 - k, d], row_id(row_far[k]))

    def col_copy(k):
        back = len(col_far) - 1 - k
        return remote(mine, cols.at[back], col_send.at[back], col_recv.at[back],
                      col_id(col_far[k]))

    if relay:
        for d in range(disp):
            load_tile(d)
            if d == 0:
                pl.semaphore_wait(barrier, len(greeted))
            first_copy(d).start()
            own_copy(d).start()
    else:
        for d in range(disp):
            load_tile(d)
        pl.semaphore_wait(barrier, len(greeted))
        for d in range(disp):
            for k in range(len(row_far)):
                row_copy(k, d).start()

    loads[disp].wait()
    mask_blocks(strip, p0_occ, c * col_blocks - half, c * col_blocks, total)
    owner = r * row_blocks // col_blocks
    offset = pl.multiple_of((r * row_blocks - owner * col_blocks) * BLK, BLK)

    def fact_copy(k):
        return remote(fact, fact, fact_send.at[k], fact_recv.at[0], col_id(k + 1))

    core_odd = lax.rem(c, 2)
    core = col_id(1 - 2 * core_odd)
    across = lax.rem(owner + 2, col_count)

    def fact_core():
        return remote(fact, fact, fact_send.at[0], fact_recv.at[0], core)

    def fact_across():
        return remote(fact, fact, fact_send.at[1], fact_recv.at[0], col_id(2))

    def col_core():
        return remote(mine, cols.at[core_odd], col_send.at[0], col_recv.at[0], core)

    def col_across():
        return remote(mine, cols.at[1 - core_odd], col_send.at[1], col_recv.at[1],
                      col_id(2 * core_odd - 1))

    @pl.when(c == owner)
    def _():
        for k in range(fact.shape[1] // BLK):
            for i in range(row_blocks):
                block = strip[pl.ds(offset + k * BLK, BLK), pl.ds(offset + i * BLK, BLK)]
                fact[i * BLK:(i + 1) * BLK, k * BLK:(k + 1) * BLK] = block.T
        if relay:
            fact_across().start()
            fact_core().start()
        else:
            for k in range(col_count - 1):
                fact_copy(k).start()

    if relay:
        col_core().start()
    else:
        for k in range(len(col_far)):
            col_copy(k).start()

    def col_add(tile, distance, first=False):
        at = pl.ds(pl.multiple_of((distance + col_span) * width, BLK), width)

        def step(d, carry):
            term = jnp.dot(tile[d], strip[at, :], preferred_element_type=jnp.float32)
            acc[d] = term if first else acc[d] + term
            return carry

        lax.fori_loop(0, disp, step, 0)

    def row_term(tile, distance, d):
        at = pl.ds(pl.multiple_of((distance + row_span) * height, BLK), height)
        return jnp.dot(fact[:, at], tile[d], preferred_element_type=jnp.float32)

    def row_add(tile, distance):
        def step(d, carry):
            acc[d] += row_term(tile, distance, d)
            return carry

        lax.fori_loop(0, disp, step, 0)

    def finish(d):
        squared = branch[d].astype(jnp.float32)
        for i in range(row_blocks):
            for j in range(col_blocks):
                at = (d, slice(i * BLK, (i + 1) * BLK), slice(j * BLK, (j + 1) * BLK))
                weight = p1_occ[r * row_blocks + i, c * col_blocks + j].astype(jnp.float32)
                own = mine[at].astype(jnp.float32) * (2.0 - 2.0 * squared)
                value = own + acc[at] * (2.0 * squared - 1.0)
                out[at] = (value * weight).astype(jnp.bfloat16)

    def wait_fact():
        @pl.when(c != owner)
        def _():
            fact_copy(0).wait_recv()

        if relay:
            @pl.when(c == across)
            def _():
                fact_core().start()

    col_add(mine, 0, first=True)
    if relay:
        def forward(d):
            first_copy(d).wait_recv()
            relay_copy(d).start()

        col_core().wait_recv()
        col_add(cols.at[1 - core_odd], 1 - 2 * core_odd)
        forward(0)
        col_across().start()
        wait_fact()
        row_add(mine, 0)
        forward(1)
        first_copy(1).wait_send()
        last_copy(0).start()
        forward(2)
        first_copy(2).wait_send()
        for d in range(1, disp):
            last_copy(d).start()
        for d in range(disp):
            own_copy(d).wait_recv()
        row_add(rows.at[2 - odd], 1 - 2 * odd)
        row_add(rows.at[3 - 3 * odd], 2 - 4 * odd)
        col_across().wait_recv()
        col_add(cols.at[core_odd], 2 * core_odd - 1)
        for d in range(disp):
            last_copy(d).wait_recv()
            acc[d] += row_term(rows.at[3 * odd], 4 * odd - 2, d)
            relay_copy(d).wait_recv()
            acc[d] += row_term(rows.at[1 + odd], 2 * odd - 1, d)
            finish(d)
    else:
        wait_fact()
        row_add(mine, 0)
        for k in range(len(col_far)):
            col_copy(k).wait_recv()
            col_add(cols.at[len(col_far) - 1 - k], col_far[len(col_far) - 1 - k])
        for k in range(len(row_far)):
            for d in range(disp):
                row_copy(k, d).wait_recv()
            row_add(rows.at[len(row_far) - 1 - k], row_far[len(row_far) - 1 - k])
        for d in range(disp):
            finish(d)

    if relay:
        col_core().wait_send()
        col_across().wait_send()
        first_copy(0).wait_send()
        for d in range(disp):
            last_copy(d).wait_send()
            own_copy(d).wait_send()
            relay_copy(d).wait_send()

        @pl.when(c == owner)
        def _():
            fact_across().wait_send()

        @pl.when(jnp.logical_or(c == owner, c == across))
        def _():
            fact_core().wait_send()
    else:
        for k in range(len(col_far)):
            col_copy(k).wait_send()
        for d in range(disp):
            for k in range(len(row_far)):
                row_copy(k, d).wait_send()

        @pl.when(c == owner)
        def _():
            for k in range(col_count - 1):
                fact_copy(k).wait_send()


def body(sp2_branch, p0_occupancy, p1_occupancy, p0_columns, p1_tiles):
    row_count, col_count = lax.axis_size("row"), lax.axis_size("col")
    disp, height, width = p1_tiles.shape
    strip_rows = p0_columns.shape[0]
    half = (strip_rows - width) // 2
    row_slots, col_slots = 2 * (half // height), 2 * (half // width)
    bf16 = jnp.bfloat16
    relay = row_slots == 4 and col_slots == 2 and col_count == 4 and disp == 3
    flops = 2 * disp * height * width * (strip_rows + height + 2 * half)
    return pl.pallas_call(
        functools.partial(kernel, row_count, col_count, relay),
        out_shape=pltpu.VMEM(p1_tiles.shape, bf16),
        in_specs=[pl.BlockSpec(memory_space=pltpu.SMEM)] * 3
        + [pl.BlockSpec(memory_space=pl.ANY)] * 2,
        out_specs=pl.BlockSpec(memory_space=pltpu.VMEM),
        scratch_shapes=[
            pltpu.SemaphoreType.DMA((disp + 1,)),
            pltpu.VMEM((disp, height, width), bf16),
            pltpu.VMEM(p0_columns.shape, bf16),
            pltpu.VMEM((height, height + 2 * half), bf16),
            pltpu.VMEM((disp, height, width), jnp.float32),
            pltpu.VMEM((col_slots, disp, height, width), bf16),
            pltpu.VMEM((row_slots, disp, height, width), bf16),
            pltpu.SemaphoreType.DMA((col_slots,)),
            pltpu.SemaphoreType.DMA((col_slots,)),
            pltpu.SemaphoreType.DMA((row_slots, disp)),
            pltpu.SemaphoreType.DMA((row_slots, disp)),
            pltpu.SemaphoreType.DMA((col_count - 1,)),
            pltpu.SemaphoreType.DMA((1,)),
        ],
        compiler_params=pltpu.CompilerParams(
            collective_id=0, has_side_effects=True, vmem_limit_bytes=58 * 1024 * 1024
        ),
        cost_estimate=pl.CostEstimate(flops=flops, bytes_accessed=4 << 20, transcendentals=0),
    )(sp2_branch, p0_occupancy, p1_occupancy, p0_columns, p1_tiles)


def solution(mesh):
    in_specs = (P(), P(), P(), P("col", None), P(None, "row", "col"))
    out_specs = P(None, "row", "col")
    return jax.shard_map(body, mesh=mesh, in_specs=in_specs, out_specs=out_specs, check_vma=False)
```

```python
import functools

import jax
import jax.numpy as jnp
from jax import lax
from jax.experimental import pallas as pl
from jax.experimental.pallas import tpu as pltpu
from jax.sharding import PartitionSpec as P

BLK = 256
MESH = pl.DeviceIdType.MESH


def mask_blocks(values, occ, row_block, col_block, total):
    rows, cols = values.shape
    for i in range(rows // BLK):
        for j in range(cols // BLK):
            weight = occ[lax.rem(row_block + i + total, total), col_block + j].astype(jnp.float32)
            at = (slice(i * BLK, (i + 1) * BLK), slice(j * BLK, (j + 1) * BLK))
            values[at] = (values[at].astype(jnp.float32) * weight).astype(jnp.bfloat16)


def kernel(
    row_count, col_count, relay,
    branch, p0_occ, p1_occ, strip_in, tile_in, out,
    load_sem, mine, strip, fact, acc, cols, rows,
    col_send, col_recv, row_send, row_recv, fact_send, fact_recv,
):
    disp, height, width = tile_in.shape
    row_blocks, col_blocks = height // BLK, width // BLK
    total = col_count * col_blocks
    half = (strip_in.shape[0] // BLK - col_blocks) // 2
    col_span, row_span = half // col_blocks, half // row_blocks
    r, c = lax.axis_index("row"), lax.axis_index("col")
    odd = lax.rem(r, 2)

    def row_id(distance):
        return (lax.rem(r + distance + row_count, row_count), c)

    def col_id(distance):
        return (r, lax.rem(c + distance + col_count, col_count))

    row_far = [t for t in range(-row_span, row_span + 1) if t]
    col_far = [t for t in range(-col_span, col_span + 1) if t]
    partner = row_id(1 - 2 * odd)
    greeted = [col_id(t) for t in range(1, col_count)]
    greeted += [row_id(2), row_id(-2), partner] if relay else [row_id(t) for t in row_far]
    barrier = pltpu.get_barrier_semaphore()
    for device in greeted:
        pl.semaphore_signal(barrier, inc=1, device_id=device, device_id_type=MESH)

    loads = [pltpu.make_async_copy(tile_in.at[d], mine.at[d], load_sem.at[d]) for d in range(disp)]
    loads.append(pltpu.make_async_copy(strip_in, strip, load_sem.at[disp]))
    for load in loads:
        load.start()

    def load_tile(d):
        loads[d].wait()
        mask_blocks(mine.at[d], p1_occ, r * row_blocks, c * col_blocks, total)

    def remote(src, dst, send, recv, device):
        return pltpu.make_async_remote_copy(
            src_ref=src, dst_ref=dst, send_sem=send, recv_sem=recv,
            device_id=device, device_id_type=MESH,
        )

    def first_copy(d):
        return remote(mine.at[d], rows.at[3 - 3 * odd, d], row_send.at[0, d],
                      row_recv.at[0, d], row_id(4 * odd - 2))

    def last_copy(d):
        return remote(mine.at[d], rows.at[3 * odd, d], row_send.at[1, d],
                      row_recv.at[1, d], row_id(2 - 4 * odd))

    def own_copy(d):
        return remote(mine.at[d], rows.at[1 + odd, d], row_send.at[2, d],
                      row_recv.at[2, d], partner)

    def relay_copy(d):
        return remote(rows.at[3 - 3 * odd, d], rows.at[2 - odd, d], row_send.at[3, d],
                      row_recv.at[3, d], partner)

    def row_copy(k, d):
        return remote(mine.at[d], rows.at[len(row_far) - 1 - k, d],
                      row_send.at[len(row_far) - 1 - k, d],
                      row_recv.at[len(row_far) - 1 - k, d], row_id(row_far[k]))

    def col_copy(k):
        back = len(col_far) - 1 - k
        return remote(mine, cols.at[back], col_send.at[back], col_recv.at[back],
                      col_id(col_far[k]))

    if relay:
        for d in range(disp):
            load_tile(d)
            if d == 0:
                pl.semaphore_wait(barrier, len(greeted))
            first_copy(d).start()
            own_copy(d).start()
    else:
        for d in range(disp):
            load_tile(d)
        pl.semaphore_wait(barrier, len(greeted))
        for d in range(disp):
            for k in range(len(row_far)):
                row_copy(k, d).start()

    loads[disp].wait()
    mask_blocks(strip, p0_occ, c * col_blocks - half, c * col_blocks, total)
    owner = r * row_blocks // col_blocks
    offset = pl.multiple_of((r * row_blocks - owner * col_blocks) * BLK, BLK)

    def fact_copy(k):
        return remote(fact, fact, fact_send.at[k], fact_recv.at[0], col_id(k + 1))

    core_odd = lax.rem(c, 2)
    core = col_id(1 - 2 * core_odd)
    across = lax.rem(owner + 2, col_count)

    def fact_core():
        return remote(fact, fact, fact_send.at[0], fact_recv.at[0], core)

    def fact_across():
        return remote(fact, fact, fact_send.at[1], fact_recv.at[0], col_id(2))

    def col_core():
        return remote(mine, cols.at[core_odd], col_send.at[0], col_recv.at[0], core)

    def col_across():
        return remote(mine, cols.at[1 - core_odd], col_send.at[1], col_recv.at[1],
                      col_id(2 * core_odd - 1))

    @pl.when(c == owner)
    def _():
        for k in range(fact.shape[1] // BLK):
            for i in range(row_blocks):
                block = strip[pl.ds(offset + k * BLK, BLK), pl.ds(offset + i * BLK, BLK)]
                fact[i * BLK:(i + 1) * BLK, k * BLK:(k + 1) * BLK] = block.T
        if relay:
            fact_across().start()
            fact_core().start()
        else:
            for k in range(col_count - 1):
                fact_copy(k).start()

    if relay:
        col_core().start()
    else:
        for k in range(len(col_far)):
            col_copy(k).start()

    def col_add(tile, distance, first=False):
        at = pl.ds(pl.multiple_of((distance + col_span) * width, BLK), width)

        def step(d, carry):
            term = jnp.dot(tile[d], strip[at, :], preferred_element_type=jnp.float32)
            acc[d] = term if first else acc[d] + term
            return carry

        lax.fori_loop(0, disp, step, 0)

    def row_term(tile, distance, d):
        at = pl.ds(pl.multiple_of((distance + row_span) * height, BLK), height)
        return jnp.dot(fact[:, at], tile[d], preferred_element_type=jnp.float32)

    def row_add(tile, distance):
        def step(d, carry):
            acc[d] += row_term(tile, distance, d)
            return carry

        lax.fori_loop(0, disp, step, 0)

    def finish(d):
        squared = branch[d].astype(jnp.float32)
        for i in range(row_blocks):
            for j in range(col_blocks):
                at = (d, slice(i * BLK, (i + 1) * BLK), slice(j * BLK, (j + 1) * BLK))
                weight = p1_occ[r * row_blocks + i, c * col_blocks + j].astype(jnp.float32)
                own = mine[at].astype(jnp.float32) * (2.0 - 2.0 * squared)
                value = own + acc[at] * (2.0 * squared - 1.0)
                out[at] = (value * weight).astype(jnp.bfloat16)

    def wait_fact():
        @pl.when(c != owner)
        def _():
            fact_copy(0).wait_recv()

        if relay:
            @pl.when(c == across)
            def _():
                fact_core().start()

    col_add(mine, 0, first=True)
    if relay:
        def forward(d):
            first_copy(d).wait_recv()
            relay_copy(d).start()

        col_core().wait_recv()
        col_add(cols.at[1 - core_odd], 1 - 2 * core_odd)
        for d in range(disp):
            forward(d)
            last_copy(d).start()
            if d == 0:
                col_across().start()
            if d == 1:
                wait_fact()
                row_add(mine, 0)
        for d in range(disp):
            own_copy(d).wait_recv()
        row_add(rows.at[2 - odd], 1 - 2 * odd)
        row_add(rows.at[3 - 3 * odd], 2 - 4 * odd)
        col_across().wait_recv()
        col_add(cols.at[core_odd], 2 * core_odd - 1)
        for d in range(disp):
            last_copy(d).wait_recv()
            acc[d] += row_term(rows.at[3 * odd], 4 * odd - 2, d)
            relay_copy(d).wait_recv()
            acc[d] += row_term(rows.at[1 + odd], 2 * odd - 1, d)
            finish(d)
    else:
        wait_fact()
        row_add(mine, 0)
        for k in range(len(col_far)):
            col_copy(k).wait_recv()
            col_add(cols.at[len(col_far) - 1 - k], col_far[len(col_far) - 1 - k])
        for k in range(len(row_far)):
            for d in range(disp):
                row_copy(k, d).wait_recv()
            row_add(rows.at[len(row_far) - 1 - k], row_far[len(row_far) - 1 - k])
        for d in range(disp):
            finish(d)

    if relay:
        col_core().wait_send()
        col_across().wait_send()
        for d in range(disp):
            first_copy(d).wait_send()
            last_copy(d).wait_send()
            own_copy(d).wait_send()
            relay_copy(d).wait_send()

        @pl.when(c == owner)
        def _():
            fact_across().wait_send()

        @pl.when(jnp.logical_or(c == owner, c == across))
        def _():
            fact_core().wait_send()
    else:
        for k in range(len(col_far)):
            col_copy(k).wait_send()
        for d in range(disp):
            for k in range(len(row_far)):
                row_copy(k, d).wait_send()

        @pl.when(c == owner)
        def _():
            for k in range(col_count - 1):
                fact_copy(k).wait_send()


def body(sp2_branch, p0_occupancy, p1_occupancy, p0_columns, p1_tiles):
    row_count, col_count = lax.axis_size("row"), lax.axis_size("col")
    disp, height, width = p1_tiles.shape
    strip_rows = p0_columns.shape[0]
    half = (strip_rows - width) // 2
    row_slots, col_slots = 2 * (half // height), 2 * (half // width)
    bf16 = jnp.bfloat16
    relay = row_slots == 4 and col_slots == 2 and col_count == 4 and disp == 3
    flops = 2 * disp * height * width * (strip_rows + height + 2 * half)
    return pl.pallas_call(
        functools.partial(kernel, row_count, col_count, relay),
        out_shape=pltpu.VMEM(p1_tiles.shape, bf16),
        in_specs=[pl.BlockSpec(memory_space=pltpu.SMEM)] * 3
        + [pl.BlockSpec(memory_space=pl.ANY)] * 2,
        out_specs=pl.BlockSpec(memory_space=pltpu.VMEM),
        scratch_shapes=[
            pltpu.SemaphoreType.DMA((disp + 1,)),
            pltpu.VMEM((disp, height, width), bf16),
            pltpu.VMEM(p0_columns.shape, bf16),
            pltpu.VMEM((height, height + 2 * half), bf16),
            pltpu.VMEM((disp, height, width), jnp.float32),
            pltpu.VMEM((col_slots, disp, height, width), bf16),
            pltpu.VMEM((row_slots, disp, height, width), bf16),
            pltpu.SemaphoreType.DMA((col_slots,)),
            pltpu.SemaphoreType.DMA((col_slots,)),
            pltpu.SemaphoreType.DMA((row_slots, disp)),
            pltpu.SemaphoreType.DMA((row_slots, disp)),
            pltpu.SemaphoreType.DMA((col_count - 1,)),
            pltpu.SemaphoreType.DMA((1,)),
        ],
        compiler_params=pltpu.CompilerParams(
            collective_id=0, has_side_effects=True, vmem_limit_bytes=58 * 1024 * 1024
        ),
        cost_estimate=pl.CostEstimate(flops=flops, bytes_accessed=4 << 20, transcendentals=0),
    )(sp2_branch, p0_occupancy, p1_occupancy, p0_columns, p1_tiles)


def solution(mesh):
    in_specs = (P(), P(), P(), P("col", None), P(None, "row", "col"))
    out_specs = P(None, "row", "col")
    return jax.shard_map(body, mesh=mesh, in_specs=in_specs, out_specs=out_specs, check_vma=False)
```

```python
import functools

import jax
import jax.numpy as jnp
from jax import lax
from jax.experimental import pallas as pl
from jax.experimental.pallas import tpu as pltpu
from jax.sharding import PartitionSpec as P

BLK = 256
MESH = pl.DeviceIdType.MESH


def mask_blocks(values, occ, row_block, col_block, total):
    rows, cols = values.shape
    for i in range(rows // BLK):
        for j in range(cols // BLK):
            weight = occ[lax.rem(row_block + i + total, total), col_block + j].astype(jnp.float32)
            at = (slice(i * BLK, (i + 1) * BLK), slice(j * BLK, (j + 1) * BLK))
            values[at] = (values[at].astype(jnp.float32) * weight).astype(jnp.bfloat16)


def kernel(
    row_count, col_count, relay,
    branch, p0_occ, p1_occ, strip_in, tile_in, out,
    load_sem, mine, strip, fact, acc, cols, rows,
    col_send, col_recv, row_send, row_recv, fact_send, fact_recv,
):
    disp, height, width = tile_in.shape
    row_blocks, col_blocks = height // BLK, width // BLK
    total = col_count * col_blocks
    half = (strip_in.shape[0] // BLK - col_blocks) // 2
    col_span, row_span = half // col_blocks, half // row_blocks
    r, c = lax.axis_index("row"), lax.axis_index("col")
    odd = lax.rem(r, 2)

    def row_id(distance):
        return (lax.rem(r + distance + row_count, row_count), c)

    def col_id(distance):
        return (r, lax.rem(c + distance + col_count, col_count))

    row_far = [t for t in range(-row_span, row_span + 1) if t]
    col_far = [t for t in range(-col_span, col_span + 1) if t]
    partner = row_id(1 - 2 * odd)
    greeted = [col_id(t) for t in range(1, col_count)]
    greeted += [row_id(2), row_id(-2), partner] if relay else [row_id(t) for t in row_far]
    barrier = pltpu.get_barrier_semaphore()
    for device in greeted:
        pl.semaphore_signal(barrier, inc=1, device_id=device, device_id_type=MESH)

    loads = [pltpu.make_async_copy(tile_in.at[d], mine.at[d], load_sem.at[d]) for d in range(disp)]
    loads.append(pltpu.make_async_copy(strip_in, strip, load_sem.at[disp]))
    for load in loads:
        load.start()

    def load_tile(d):
        loads[d].wait()
        mask_blocks(mine.at[d], p1_occ, r * row_blocks, c * col_blocks, total)

    def remote(src, dst, send, recv, device):
        return pltpu.make_async_remote_copy(
            src_ref=src, dst_ref=dst, send_sem=send, recv_sem=recv,
            device_id=device, device_id_type=MESH,
        )

    def first_copy(d):
        return remote(mine.at[d], rows.at[3 - 3 * odd, d], row_send.at[0, d],
                      row_recv.at[0, d], row_id(4 * odd - 2))

    def last_copy(d):
        return remote(mine.at[d], rows.at[3 * odd, d], row_send.at[1, d],
                      row_recv.at[1, d], row_id(2 - 4 * odd))

    def own_copy(d):
        return remote(mine.at[d], rows.at[1 + odd, d], row_send.at[2, d],
                      row_recv.at[2, d], partner)

    def relay_copy(d):
        return remote(rows.at[3 - 3 * odd, d], rows.at[2 - odd, d], row_send.at[3, d],
                      row_recv.at[3, d], partner)

    def row_copy(k, d):
        return remote(mine.at[d], rows.at[len(row_far) - 1 - k, d],
                      row_send.at[len(row_far) - 1 - k, d],
                      row_recv.at[len(row_far) - 1 - k, d], row_id(row_far[k]))

    def col_copy(k):
        back = len(col_far) - 1 - k
        return remote(mine, cols.at[back], col_send.at[back], col_recv.at[back],
                      col_id(col_far[k]))

    if relay:
        for d in range(disp):
            load_tile(d)
            if d == 0:
                pl.semaphore_wait(barrier, len(greeted))
            first_copy(d).start()
            own_copy(d).start()
    else:
        for d in range(disp):
            load_tile(d)
        pl.semaphore_wait(barrier, len(greeted))
        for d in range(disp):
            for k in range(len(row_far)):
                row_copy(k, d).start()

    loads[disp].wait()
    mask_blocks(strip, p0_occ, c * col_blocks - half, c * col_blocks, total)
    owner = r * row_blocks // col_blocks
    offset = pl.multiple_of((r * row_blocks - owner * col_blocks) * BLK, BLK)

    def fact_copy(k):
        return remote(fact, fact, fact_send.at[k], fact_recv.at[0], col_id(k + 1))

    core_odd = lax.rem(c, 2)
    core = col_id(1 - 2 * core_odd)
    across = lax.rem(owner + 2, col_count)

    def fact_core():
        return remote(fact, fact, fact_send.at[0], fact_recv.at[0], core)

    def fact_across():
        return remote(fact, fact, fact_send.at[1], fact_recv.at[0], col_id(2))

    def col_core():
        return remote(mine, cols.at[core_odd], col_send.at[0], col_recv.at[0], core)

    def col_across():
        return remote(mine, cols.at[1 - core_odd], col_send.at[1], col_recv.at[1],
                      col_id(2 * core_odd - 1))

    @pl.when(c == owner)
    def _():
        for k in range(fact.shape[1] // BLK):
            for i in range(row_blocks):
                block = strip[pl.ds(offset + k * BLK, BLK), pl.ds(offset + i * BLK, BLK)]
                fact[i * BLK:(i + 1) * BLK, k * BLK:(k + 1) * BLK] = block.T
        if relay:
            fact_across().start()
            fact_core().start()
        else:
            for k in range(col_count - 1):
                fact_copy(k).start()

    if relay:
        col_core().start()
        col_across().start()
    else:
        for k in range(len(col_far)):
            col_copy(k).start()

    def col_add(tile, distance, first=False):
        at = pl.ds(pl.multiple_of((distance + col_span) * width, BLK), width)

        def step(d, carry):
            term = jnp.dot(tile[d], strip[at, :], preferred_element_type=jnp.float32)
            acc[d] = term if first else acc[d] + term
            return carry

        lax.fori_loop(0, disp, step, 0)

    def row_term(tile, distance, d):
        at = pl.ds(pl.multiple_of((distance + row_span) * height, BLK), height)
        return jnp.dot(fact[:, at], tile[d], preferred_element_type=jnp.float32)

    def row_add(tile, distance):
        def step(d, carry):
            acc[d] += row_term(tile, distance, d)
            return carry

        lax.fori_loop(0, disp, step, 0)

    def finish(d):
        squared = branch[d].astype(jnp.float32)
        for i in range(row_blocks):
            for j in range(col_blocks):
                at = (d, slice(i * BLK, (i + 1) * BLK), slice(j * BLK, (j + 1) * BLK))
                weight = p1_occ[r * row_blocks + i, c * col_blocks + j].astype(jnp.float32)
                own = mine[at].astype(jnp.float32) * (2.0 - 2.0 * squared)
                value = own + acc[at] * (2.0 * squared - 1.0)
                out[at] = (value * weight).astype(jnp.bfloat16)

    def wait_fact():
        @pl.when(c != owner)
        def _():
            fact_copy(0).wait_recv()

        if relay:
            @pl.when(c == across)
            def _():
                fact_core().start()

    col_add(mine, 0, first=True)
    if relay:
        def forward(d):
            first_copy(d).wait_recv()
            relay_copy(d).start()

        col_core().wait_recv()
        col_add(cols.at[1 - core_odd], 1 - 2 * core_odd)
        for d in range(disp):
            forward(d)
            last_copy(d).start()
            if d == 1:
                wait_fact()
                row_add(mine, 0)
        for d in range(disp):
            own_copy(d).wait_recv()
        row_add(rows.at[2 - odd], 1 - 2 * odd)
        row_add(rows.at[3 - 3 * odd], 2 - 4 * odd)
        col_across().wait_recv()
        col_add(cols.at[core_odd], 2 * core_odd - 1)
        for d in range(disp):
            last_copy(d).wait_recv()
            acc[d] += row_term(rows.at[3 * odd], 4 * odd - 2, d)
            relay_copy(d).wait_recv()
            acc[d] += row_term(rows.at[1 + odd], 2 * odd - 1, d)
            finish(d)
    else:
        wait_fact()
        row_add(mine, 0)
        for k in range(len(col_far)):
            col_copy(k).wait_recv()
            col_add(cols.at[len(col_far) - 1 - k], col_far[len(col_far) - 1 - k])
        for k in range(len(row_far)):
            for d in range(disp):
                row_copy(k, d).wait_recv()
            row_add(rows.at[len(row_far) - 1 - k], row_far[len(row_far) - 1 - k])
        for d in range(disp):
            finish(d)

    if relay:
        col_core().wait_send()
        col_across().wait_send()
        for d in range(disp):
            first_copy(d).wait_send()
            last_copy(d).wait_send()
            own_copy(d).wait_send()
            relay_copy(d).wait_send()

        @pl.when(c == owner)
        def _():
            fact_across().wait_send()

        @pl.when(jnp.logical_or(c == owner, c == across))
        def _():
            fact_core().wait_send()
    else:
        for k in range(len(col_far)):
            col_copy(k).wait_send()
        for d in range(disp):
            for k in range(len(row_far)):
                row_copy(k, d).wait_send()

        @pl.when(c == owner)
        def _():
            for k in range(col_count - 1):
                fact_copy(k).wait_send()


def body(sp2_branch, p0_occupancy, p1_occupancy, p0_columns, p1_tiles):
    row_count, col_count = lax.axis_size("row"), lax.axis_size("col")
    disp, height, width = p1_tiles.shape
    strip_rows = p0_columns.shape[0]
    half = (strip_rows - width) // 2
    row_slots, col_slots = 2 * (half // height), 2 * (half // width)
    bf16 = jnp.bfloat16
    relay = row_slots == 4 and col_slots == 2 and col_count == 4 and disp == 3
    flops = 2 * disp * height * width * (strip_rows + height + 2 * half)
    return pl.pallas_call(
        functools.partial(kernel, row_count, col_count, relay),
        out_shape=pltpu.VMEM(p1_tiles.shape, bf16),
        in_specs=[pl.BlockSpec(memory_space=pltpu.SMEM)] * 3
        + [pl.BlockSpec(memory_space=pl.ANY)] * 2,
        out_specs=pl.BlockSpec(memory_space=pltpu.VMEM),
        scratch_shapes=[
            pltpu.SemaphoreType.DMA((disp + 1,)),
            pltpu.VMEM((disp, height, width), bf16),
            pltpu.VMEM(p0_columns.shape, bf16),
            pltpu.VMEM((height, height + 2 * half), bf16),
            pltpu.VMEM((disp, height, width), jnp.float32),
            pltpu.VMEM((col_slots, disp, height, width), bf16),
            pltpu.VMEM((row_slots, disp, height, width), bf16),
            pltpu.SemaphoreType.DMA((col_slots,)),
            pltpu.SemaphoreType.DMA((col_slots,)),
            pltpu.SemaphoreType.DMA((row_slots, disp)),
            pltpu.SemaphoreType.DMA((row_slots, disp)),
            pltpu.SemaphoreType.DMA((col_count - 1,)),
            pltpu.SemaphoreType.DMA((1,)),
        ],
        compiler_params=pltpu.CompilerParams(
            collective_id=0, has_side_effects=True, vmem_limit_bytes=58 * 1024 * 1024
        ),
        cost_estimate=pl.CostEstimate(flops=flops, bytes_accessed=4 << 20, transcendentals=0),
    )(sp2_branch, p0_occupancy, p1_occupancy, p0_columns, p1_tiles)


def solution(mesh):
    in_specs = (P(), P(), P(), P("col", None), P(None, "row", "col"))
    out_specs = P(None, "row", "col")
    return jax.shard_map(body, mesh=mesh, in_specs=in_specs, out_specs=out_specs, check_vma=False)
```
